32 devices in a mesh: groups: 2 (over x), dp: 8 (over z, y), mp: 2 (over core).
Axes of the slice: x: 2, y: 2, z: 4, core: 2. Of those that a mesh axis runs over, the one named last changes fastest.
Arguments:
- frozen_state: bfloat16 [32, 128, 4096], P(('groups', 'dp', 'mp')), parts along dimension 0, may hold values from -6 to 6
- gated_hidden: bfloat16 [32, 128, 14336], P(('groups', 'dp', 'mp')), parts along dimension 0, may hold values from -4 to 4
- lengths: int32 [32], P(('groups', 'dp', 'mp')), parts along dimension 0, may hold values from 1 to 128, as said below
- positives: int32 [32], P('groups'), parts along dimension 0, may hold values from 0 to 15, as said below
- adapter_down_factor: bfloat16 [16, 14336], replicated, may hold values from -0.046875 to 0.046875
- adapter_up_factor: bfloat16 [16, 4096], replicated, may hold values from -1.5 to 1.5
- final_norm_weight: float32 [4096], replicated, may hold values from 0.5 to 1.5
Outputs:
- grad_down: float32 [32, 14336], P('groups', 'mp'), parts along dimension 0
- grad_up: float32 [32, 4096], P('groups', 'mp'), parts along dimension 0
- mean_loss: float32 [2], P('groups'), parts along dimension 0
The draws below stay inside these ranges and needn't reach their ends.
There are 2 independent parts, one for each index of `groups`. The reference program is written for one: setup_inputs(seed, part) draws one part's arguments, and reference() takes and returns one part's arrays. A program takes and returns all parts, laid end to end along the dimension named above; an argument that names none is the same for every part. Nothing has to cross between parts.
Inputs may be any that keep to these rules, and one draw needn't show every extreme that they name: lengths are 1 to 128; passage 0 is unpadded. `positives`: positives_i != i.
All inputs are finite; a program needn't handle non-finite values.
Results may differ from the reference program's by a relative error of at most 0.0045.
Values sent between devices are 32-bit elements; how exact they have to be, the bound alone decides.
A program may use at most 64 MiB of HBM per device.

```python
import jax
import jax.numpy as jnp
from jax import lax

MODEL_WIDTH = 4096
HIDDEN_UNITS = 14336
ADAPTER_RANK = 16
PSG_LEN = 128
PASSAGES = 16


def draw_lengths(key, part):
    key = jax.random.fold_in(key, 11)
    values = jax.random.randint(key, (PASSAGES,), 1, PSG_LEN + 1, dtype=jnp.int32)
    places = jnp.arange(PASSAGES, dtype=jnp.int32)
    return jnp.where(places == 0, PSG_LEN, values).astype(jnp.int32)


def draw_positives(key, part):
    key = jax.random.fold_in(key, 23)
    offsets = jax.random.randint(key, (PASSAGES,), 1, PASSAGES, dtype=jnp.int32)
    places = jnp.arange(PASSAGES, dtype=jnp.int32)
    offsets = jnp.where(places < 2, PASSAGES - 1, offsets)
    return ((places + offsets) % PASSAGES).astype(jnp.int32)


def block_levels(rng, extent, split, least, largest):
    def one(position, blocks):
        heights = jax.random.uniform(jax.random.fold_in(jax.random.fold_in(rng, 6), position), (blocks,), jnp.float32, least / len(split), largest / len(split))
        return jnp.repeat(jnp.exp(heights), extent[position] // blocks).reshape((-1,) + (1,) * (len(extent) - position - 1))

    loudness = one(*split[0])
    for cut in split[1:]:
        loudness = loudness * one(*cut)
    return loudness


def noise(stream_key, shape, deviation, limit, shards=(), held_as=jnp.bfloat16):
    drawn = deviation * jax.random.normal(stream_key, shape, jnp.float32)
    if shards:
        drawn = drawn * block_levels(stream_key, shape, shards, -0.22, 0.18)
    return jnp.clip(drawn, -limit, limit).astype(held_as)


def setup_inputs(seed: int = 0, part: int = 0) -> dict:
    splits = jax.random.split(jax.random.key(seed), 8)
    own_keys = jax.random.split(jax.random.fold_in(splits[7], part), 8)
    frozen_state = noise(own_keys[0], (PASSAGES, PSG_LEN, MODEL_WIDTH), 1.0, 6.0, ((0, 16),))
    gated_hidden = noise(own_keys[1], (PASSAGES, PSG_LEN, HIDDEN_UNITS), 0.5, 4.0, ((0, 16),))
    lengths = draw_lengths(jax.random.fold_in(jax.random.fold_in(splits[7], part), 71), part)
    positives = draw_positives(jax.random.fold_in(jax.random.fold_in(splits[7], part), 71), part)
    adapter_down_factor = noise(splits[4], (ADAPTER_RANK, HIDDEN_UNITS), HIDDEN_UNITS ** -0.5, 0.046875)
    adapter_up_factor = noise(splits[5], (ADAPTER_RANK, MODEL_WIDTH), ADAPTER_RANK ** -0.5, 1.5)
    final_norm_weight = jnp.clip(1.0 + 0.1 * jax.random.normal(splits[6], (MODEL_WIDTH,), jnp.float32), 0.5, 1.5)
    return {"frozen_state": frozen_state, "gated_hidden": gated_hidden, "lengths": lengths, "positives": positives, "adapter_down_factor": adapter_down_factor, "adapter_up_factor": adapter_up_factor, "final_norm_weight": final_norm_weight}


EPS_NORM = 1e-05
EPS_LEN = 1e-06
TEMP = 0.05
HIGH = lax.Precision.HIGHEST

def encode_single_passage(passage_base, passage_hidden, passage_length, adapter_down_factor, adapter_up_factor, final_norm_weight):
    lowrank_projection = jnp.dot(passage_hidden, adapter_down_factor.T, preferred_element_type=jnp.float32).astype(jnp.bfloat16)
    adapted_state = passage_base.astype(jnp.float32) + jnp.dot(lowrank_projection, adapter_up_factor, preferred_element_type=jnp.float32)
    inverse_norm = lax.rsqrt(lax.optimization_barrier(jnp.mean(adapted_state * adapted_state, axis=-1, keepdims=True)) + EPS_NORM)
    places = jnp.arange(adapted_state.shape[0], dtype=jnp.int32)
    pooling_weight = jnp.where(places < passage_length, 1.0, 0.0).astype(jnp.float32) / passage_length.astype(jnp.float32)
    pooled = jnp.dot(pooling_weight, adapted_state * inverse_norm * final_norm_weight, precision=HIGH)
    return (lowrank_projection, adapted_state, inverse_norm, pooling_weight, pooled)

def reference(frozen_state, gated_hidden, lengths, positives, adapter_down_factor, adapter_up_factor, final_norm_weight):

    def fwd(args):
        passage_base, passage_hidden, passage_length = args
        return encode_single_passage(passage_base, passage_hidden, passage_length, adapter_down_factor, adapter_up_factor, final_norm_weight)[4]
    pooled = lax.map(fwd, (frozen_state, gated_hidden, lengths))
    size = jnp.sqrt(lax.optimization_barrier(jnp.sum(pooled * pooled, axis=-1, keepdims=True)) + EPS_LEN)
    embed = pooled / size
    count = embed.shape[0]
    logits = jnp.dot(embed, embed.T, precision=HIGH) / TEMP
    cols = jnp.arange(count, dtype=jnp.int32)
    itself = cols[:, None] == cols[None, :]
    target = cols[None, :] == positives[:, None]
    lse = jax.nn.logsumexp(jnp.where(itself, -jnp.inf, logits), axis=1)
    loss = lse - lax.optimization_barrier(jnp.sum(jnp.where(target, logits, 0.0), axis=1))
    prob = jnp.where(itself, 0.0, jnp.exp(logits - lse[:, None]))
    coef = prob - target.astype(jnp.float32)
    d_embed = (jnp.dot(coef, embed, precision=HIGH) + jnp.dot(coef.T, embed, precision=HIGH)) / TEMP

    def bwd(carry, args):
        passage_base, passage_hidden, passage_length, emb, scale, grad_e = args
        lowrank_projection, adapted_state, inverse_norm, pooling_weight, passage_pooled = encode_single_passage(passage_base, passage_hidden, passage_length, adapter_down_factor, adapter_up_factor, final_norm_weight)
        d_pooled = (grad_e - emb * jnp.sum(emb * grad_e)) / scale
        scaled = final_norm_weight * pooling_weight[:, None] * d_pooled[None, :]
        inner = lax.optimization_barrier(jnp.sum(adapted_state * scaled, axis=-1, keepdims=True)) / adapted_state.shape[1]
        state_gradient = (inverse_norm * scaled - adapted_state * inverse_norm * inverse_norm * inverse_norm * inner).astype(jnp.bfloat16)
        g_up = jnp.dot(lowrank_projection.T, state_gradient, preferred_element_type=jnp.float32)
        lowrank_gradient = jnp.dot(state_gradient, adapter_up_factor.T, preferred_element_type=jnp.float32).astype(jnp.bfloat16)
        g_down = jnp.dot(lowrank_gradient.T, passage_hidden, preferred_element_type=jnp.float32)
        return ((carry[0] + g_down, carry[1] + g_up), None)
    start_offset = (jnp.zeros(adapter_down_factor.shape, jnp.float32), jnp.zeros(adapter_up_factor.shape, jnp.float32))
    (grad_down, grad_up), _ = lax.scan(bwd, start_offset, (frozen_state, gated_hidden, lengths, embed, size[:, 0], d_embed))
    return (grad_down, grad_up, jnp.mean(loss).reshape(1))
```

```python
import functools
import math

import jax
import jax.numpy as jnp
from jax import lax
from jax.experimental import pallas as pl
from jax.experimental.pallas import tpu as pltpu
from jax.sharding import PartitionSpec as P

EPS_NORM = 1e-05
EPS_LEN = 1e-06
TEMP = 0.05
LANE = 128
MESH = pl.DeviceIdType.MESH
F32 = jnp.float32
BF16 = jnp.bfloat16


def plan(n, width, hidden):
    blocks = (width + hidden) // 2 // LANE
    pieces = 3 if blocks % (3 * n) == 0 else 1
    unit = n * pieces
    padded = (blocks + unit - 1) // unit * unit
    ny = max(d for d in range(1, int(math.isqrt(n)) + 1) if n % d == 0)
    return pieces, padded * LANE, ny, n // ny


def nt_dot(a, b, precision=None):
    return lax.dot_general(
        a, b, (((1,), (1,)), ((), ())), preferred_element_type=F32, precision=precision
    )


def kernel(
    n,
    hidden_chunks,
    frozen_hbm,
    hidden_hbm,
    lengths_ref,
    positives_ref,
    down_hbm,
    up_ref,
    gain_ref,
    gdown_ref,
    gup_ref,
    loss_ref,
    frozen,
    hidden,
    down,
    state,
    own,
    land,
    both,
    sib,
    ybuf,
    zbuf,
    res,
    load_sem,
    esend,
    erecv,
    fsend,
    frecv,
    ssend,
    srecv,
    ysend,
    yrecv,
    zsend,
    zrecv,
    azsend,
    azrecv,
    aysend,
    ayrecv,
):
    span, width = frozen.shape
    units = hidden.shape[1]
    rank = up_ref.shape[0]
    total = 2 * n
    rows = width // LANE
    pieces, cols, ny, nz = plan(n, width, units)
    pw = cols // pieces
    yw = pw // ny
    zw = yw // nz
    hu, hd = width // 2, units // 2
    dp = lax.axis_index("dp")
    mp = lax.axis_index("mp")
    other = 1 - mp
    me = dp * 2 + mp
    y = lax.rem(dp, ny)
    z = lax.div(dp, ny)

    cw = units // hidden_chunks
    loads = []
    for c in range(hidden_chunks):
        at = pl.ds(c * cw, cw)
        loads.append(
            (
                pltpu.make_async_copy(down_hbm.at[:, at], down.at[:, at], load_sem.at[1, c]),
                pltpu.make_async_copy(
                    hidden_hbm.at[0, :, at], hidden.at[:, at], load_sem.at[0, c]
                ),
            )
        )
    frozen_load = pltpu.make_async_copy(
        frozen_hbm.at[0], frozen, load_sem.at[0, hidden_chunks]
    )
    for pair in loads:
        for copy in pair:
            copy.start()
    frozen_load.start()

    barrier = pltpu.get_barrier_semaphore()

    def greet(k, _):
        pl.semaphore_signal(
            barrier, inc=1, device_id={"dp": lax.rem(dp + k, n)}, device_id_type=MESH
        )
        return 0

    lax.fori_loop(1, n, greet, 0)
    pl.semaphore_signal(barrier, inc=1, device_id={"mp": other}, device_id_type=MESH)

    low = jnp.zeros((span, rank), F32)
    for c in range(hidden_chunks):
        for copy in loads[c]:
            copy.wait()
        at = pl.ds(c * cw, cw)
        low = low + nt_dot(hidden[:, at], down[:, at])
    low = low.astype(BF16)
    low_t = low.astype(F32).T.astype(BF16)
    frozen_load.wait()

    tile = 512
    square = jnp.zeros((span, LANE), F32)
    for c in range(width // tile):
        at = pl.ds(c * tile, tile)
        s = frozen[:, at].astype(F32) + jnp.dot(
            low, up_ref[:, at], preferred_element_type=F32
        )
        state[:, at] = s
        for g in range(tile // LANE):
            part = s[:, g * LANE : (g + 1) * LANE]
            square = square + part * part
    inv = lax.rsqrt(jnp.sum(square, axis=1, keepdims=True) / width + EPS_NORM)
    length = lengths_ref[0]
    places = lax.broadcasted_iota(jnp.int32, (span, 1), 0)
    weight = jnp.where(places < length, 1.0, 0.0).astype(F32) / length.astype(F32)
    wi = weight * inv
    for r in range(rows):
        at = pl.ds(r * LANE, LANE)
        own[pl.ds(r, 1), :] = (
            jnp.sum(state[:, at] * wi, axis=0, keepdims=True) * gain_ref[:, at]
        )

    pl.semaphore_wait(barrier, n)

    def row(i):
        return pl.ds(pl.multiple_of(i * rows, rows), rows)

    def share(k):
        return pltpu.make_async_remote_copy(
            src_ref=own,
            dst_ref=land.at[row(me)],
            send_sem=esend.at[k],
            recv_sem=erecv.at[k],
            device_id={"dp": lax.rem(dp + k, n)},
            device_id_type=MESH,
        )

    def forward(k):
        peer = lax.rem(dp + n - k, n) * 2 + mp
        return pltpu.make_async_remote_copy(
            src_ref=land.at[row(peer)],
            dst_ref=land.at[row(peer)],
            send_sem=fsend.at[k],
            recv_sem=frecv.at[k],
            device_id={"mp": other},
            device_id_type=MESH,
        )

    def start_share(k, _):
        share(k).start()
        return 0

    lax.fori_loop(1, n, start_share, 0)
    land[row(me), :] = own[...]
    forward(0).start()

    def pass_on(k, _):
        share(k).wait_recv()
        forward(k).start()
        return 0

    lax.fori_loop(1, n, pass_on, 0)

    def arrive(k, _):
        forward(k).wait()
        return 0

    lax.fori_loop(0, n, arrive, 0)

    def sent(k, _):
        share(k).wait_send()
        return 0

    lax.fori_loop(1, n, sent, 0)

    ri = lax.broadcasted_iota(jnp.int32, (total, total), 0)
    ci = lax.broadcasted_iota(jnp.int32, (total, total), 1)
    eye = ri == ci
    if total <= 16:
        sums = [jnp.zeros((total, LANE), F32) for _ in range(total)]
        for r in range(rows):
            a = land[pl.ds(r, total, stride=rows), :]
            for j in range(total):
                sums[j] = sums[j] + a * a[j : j + 1, :]
        gram = jnp.zeros((total, total), F32)
        for j in range(total):
            gram = jnp.where(ci == j, jnp.sum(sums[j], axis=1, keepdims=True), gram)
    else:
        gram = jnp.zeros((total, total), F32)
        for r in range(rows):
            a = land[pl.ds(r, total, stride=rows), :]
            gram = gram + nt_dot(a, a, lax.Precision.HIGHEST)
    diag = jnp.where(eye, gram, 0.0)
    size_col = jnp.sqrt(jnp.sum(diag, axis=1, keepdims=True) + EPS_LEN)
    size_row = jnp.sqrt(jnp.sum(diag, axis=0, keepdims=True) + EPS_LEN)
    cosine = gram / size_col / size_row
    logits = cosine / TEMP
    masked = jnp.where(eye, -jnp.inf, logits)
    top = jnp.max(masked, axis=0, keepdims=True)
    lse = top + jnp.log(jnp.sum(jnp.exp(masked - top), axis=0, keepdims=True))
    target = ri == positives_ref[...]
    loss = lse - jnp.sum(jnp.where(target, logits, 0.0), axis=0, keepdims=True)
    loss_ref[0] = jnp.sum(loss) / total
    coef_t = jnp.where(eye, 0.0, jnp.exp(logits - lse)) - jnp.where(target, 1.0, 0.0)
    mine_row = jnp.sum(jnp.where(ri == me, coef_t, 0.0), axis=0, keepdims=True)
    picked = jnp.where(ci == me, coef_t, 0.0) + jnp.where(eye, mine_row, 0.0)
    m = jnp.sum(picked, axis=1, keepdims=True) / TEMP
    cos_me = jnp.sum(jnp.where(ci == me, cosine, 0.0), axis=1, keepdims=True)
    along = jnp.sum(m * cos_me, axis=0, keepdims=True)
    is_me = ri[:, 0:1] == me
    size_me = jnp.sum(jnp.where(is_me, size_col, 0.0), axis=0, keepdims=True)
    q = (m - jnp.where(is_me, along, 0.0)) / size_col / size_me

    scaled = []
    inner = jnp.zeros((span, LANE), F32)
    for r in range(rows):
        at = pl.ds(r * LANE, LANE)
        a = land[pl.ds(r, total, stride=rows), :]
        sc = jnp.sum(a * q, axis=0, keepdims=True) * gain_ref[:, at]
        scaled.append(sc)
        inner = inner + state[:, at] * sc
    inner = jnp.sum(inner, axis=1, keepdims=True) * weight / width
    back = inv * inv * inv * inner
    dlow = jnp.zeros((span, rank), F32)
    per = tile // LANE
    for c in range(width // tile):
        at = pl.ds(c * tile, tile)
        sc = jnp.concatenate(scaled[c * per : (c + 1) * per], axis=1)
        ds = (wi * sc - state[:, at] * back).astype(BF16)
        dlow = dlow + nt_dot(ds, up_ref[:, at])
        half, col = divmod(c * tile, hu)
        both[half, :, pl.ds(col, tile)] = jnp.dot(low_t, ds, preferred_element_type=F32)
    dlow_t = dlow.astype(BF16).astype(F32).T.astype(BF16)

    def compute_piece(p, half):
        lo, hi = max(p * pw, hu), min((p + 1) * pw, hu + hd)
        while lo < hi:
            w = min(1024, hi - lo)
            at = pl.ds(pl.multiple_of(half * hd + (lo - hu), LANE), w)
            both[half, :, pl.ds(lo, w)] = jnp.dot(
                dlow_t, hidden[:, at], preferred_element_type=F32
            )
            lo += w
        lo = max(p * pw, hu + hd)
        if lo < (p + 1) * pw:
            both[half, :, pl.ds(lo, (p + 1) * pw - lo)] = jnp.zeros(
                (rank, (p + 1) * pw - lo), F32
            )

    waits = []

    def to_sibling(p):
        at = pl.ds(p * pw, pw)
        return pltpu.make_async_remote_copy(
            src_ref=both.at[other, :, at],
            dst_ref=sib.at[:, at],
            send_sem=ssend.at[p],
            recv_sem=srecv.at[p],
            device_id={"mp": other},
            device_id_type=MESH,
        )

    def chunk(base, size, index):
        return pl.ds(pl.multiple_of(base + index * size, LANE), size)

    def along_y(p, k):
        to = lax.rem(y + k, ny)
        return pltpu.make_async_remote_copy(
            src_ref=both.at[mp, :, chunk(p * pw, yw, to)],
            dst_ref=ybuf.at[p, k - 1],
            send_sem=ysend.at[p, k - 1],
            recv_sem=yrecv.at[p, k - 1],
            device_id={"dp": z * ny + to},
            device_id_type=MESH,
        )

    def along_z(p, k):
        to = lax.rem(z + k, nz)
        return pltpu.make_async_remote_copy(
            src_ref=both.at[mp, :, chunk(p * pw + y * yw, zw, to)],
            dst_ref=zbuf.at[p, k - 1],
            send_sem=zsend.at[p, k - 1],
            recv_sem=zrecv.at[p, k - 1],
            device_id={"dp": to * ny + y},
            device_id_type=MESH,
        )

    def gather_z(p, k):
        to = lax.rem(z + k, nz)
        at = chunk(p * pw + y * yw, zw, z)
        return pltpu.make_async_remote_copy(
            src_ref=res.at[:, at],
            dst_ref=res.at[:, at],
            send_sem=azsend.at[p, k - 1],
            recv_sem=azrecv.at[p, k - 1],
            device_id={"dp": to * ny + y},
            device_id_type=MESH,
        )

    def gather_y(p, k):
        to = lax.rem(y + k, ny)
        at = chunk(p * pw, yw, y)
        return pltpu.make_async_remote_copy(
            src_ref=res.at[:, at],
            dst_ref=res.at[:, at],
            send_sem=aysend.at[p, k - 1],
            recv_sem=ayrecv.at[p, k - 1],
            device_id={"dp": z * ny + to},
            device_id_type=MESH,
        )

    def start(copy):
        copy.start()
        waits.append(copy)

    for p in range(pieces):
        compute_piece(p, other)
        start(to_sibling(p))
    for p in range(pieces):
        compute_piece(p, mp)
        to_sibling(p).wait_recv()
        at = pl.ds(p * pw, pw)
        both[mp, :, at] = both[mp, :, at] + sib[:, at]
        for k in range(1, ny):
            start(along_y(p, k))
    for p in range(pieces):
        at = chunk(p * pw, yw, y)
        acc = both[mp, :, at]
        for k in range(1, ny):
            along_y(p, k).wait_recv()
            acc = acc + ybuf[p, k - 1]
        both[mp, :, at] = acc
        for k in range(1, nz):
            start(along_z(p, k))
    for p in range(pieces):
        at = chunk(p * pw + y * yw, zw, z)
        acc = both[mp, :, at]
        for k in range(1, nz):
            along_z(p, k).wait_recv()
            acc = acc + zbuf[p, k - 1]
        res[:, at] = acc
        for k in range(1, nz):
            start(gather_z(p, k))
    for p in range(pieces):
        for k in range(1, nz):
            gather_z(p, k).wait_recv()
        for k in range(1, ny):
            start(gather_y(p, k))
    for p in range(pieces):
        for k in range(1, ny):
            gather_y(p, k).wait_recv()
        lo, hi = p * pw, min((p + 1) * pw, hu)
        if lo < hi:
            gup_ref[:, pl.ds(lo, hi - lo)] = res[:, pl.ds(lo, hi - lo)]
        lo, hi = max(p * pw, hu), min((p + 1) * pw, hu + hd)
        if lo < hi:
            gdown_ref[:, pl.ds(lo - hu, hi - lo)] = res[:, pl.ds(lo, hi - lo)]
    for copy in waits:
        copy.wait_send()


def body(
    frozen_state,
    gated_hidden,
    lengths,
    positives,
    adapter_down_factor,
    adapter_up_factor,
    final_norm_weight,
    *,
    n,
):
    _, span, width = frozen_state.shape
    units = gated_hidden.shape[2]
    rank = adapter_down_factor.shape[0]
    total = positives.shape[0]
    pieces, cols, ny, nz = plan(n, width, units)
    yw = cols // pieces // ny
    zw = yw // nz
    chunks = 7
    sy, sz = max(ny - 1, 1), max(nz - 1, 1)
    dma = pltpu.SemaphoreType.DMA
    vmem = pl.BlockSpec(memory_space=pltpu.VMEM)
    smem = pl.BlockSpec(memory_space=pltpu.SMEM)
    hbm = pl.BlockSpec(memory_space=pl.ANY)
    grad_down, grad_up, mean_loss = pl.pallas_call(
        functools.partial(kernel, n, chunks),
        out_shape=(
            jax.ShapeDtypeStruct((rank, units // 2), F32),
            jax.ShapeDtypeStruct((rank, width // 2), F32),
            jax.ShapeDtypeStruct((1,), F32),
        ),
        in_specs=[hbm, hbm, smem, vmem, hbm, vmem, vmem],
        out_specs=(vmem, vmem, smem),
        scratch_shapes=[
            pltpu.VMEM((span, width), BF16),
            pltpu.VMEM((span, units), BF16),
            pltpu.VMEM((rank, units), BF16),
            pltpu.VMEM((span, width), F32),
            pltpu.VMEM((width // LANE, LANE), F32),
            pltpu.VMEM((total * (width // LANE), LANE), F32),
            pltpu.VMEM((2, rank, cols), F32),
            pltpu.VMEM((rank, cols), F32),
            pltpu.VMEM((pieces, sy, rank, yw), F32),
            pltpu.VMEM((pieces, sz, rank, zw), F32),
            pltpu.VMEM((rank, cols), F32),
            dma((2, chunks + 1)),
            dma((n,)),
            dma((n,)),
            dma((n,)),
            dma((n,)),
            dma((pieces,)),
            dma((pieces,)),
            dma((pieces, sy)),
            dma((pieces, sy)),
            dma((pieces, sz)),
            dma((pieces, sz)),
            dma((pieces, sz)),
            dma((pieces, sz)),
            dma((pieces, sy)),
            dma((pieces, sy)),
        ],
        compiler_params=pltpu.CompilerParams(
            collective_id=0, has_side_effects=True, vmem_limit_bytes=40 * 2**20
        ),
    )(
        frozen_state,
        gated_hidden,
        lengths,
        positives.reshape(1, total),
        adapter_down_factor,
        adapter_up_factor,
        final_norm_weight.reshape(1, width),
    )
    return grad_down, grad_up, mean_loss


def solution(mesh):
    in_specs = (
        P(("groups", "dp", "mp"), None, None),
        P(("groups", "dp", "mp"), None, None),
        P(("groups", "dp", "mp")),
        P("groups"),
        P(),
        P(),
        P(),
    )
    out_specs = (P("groups", "mp"), P("groups", "mp"), P("groups"))
    return jax.shard_map(
        functools.partial(body, n=mesh.shape["dp"]),
        mesh=mesh,
        in_specs=in_specs,
        out_specs=out_specs,
        check_vma=False,
    )
```

```python
import functools
import math

import jax
import jax.numpy as jnp
from jax import lax
from jax.experimental import pallas as pl
from jax.experimental.pallas import tpu as pltpu
from jax.sharding import PartitionSpec as P

EPS_NORM = 1e-05
EPS_LEN = 1e-06
TEMP = 0.05
LANE = 128
MESH = pl.DeviceIdType.MESH
F32 = jnp.float32
BF16 = jnp.bfloat16


def plan(n, width, hidden):
    blocks = (width + hidden) // 2 // LANE
    pieces = 3 if blocks % (3 * n) == 0 else 1
    unit = n * pieces
    padded = (blocks + unit - 1) // unit * unit
    ny = max(d for d in range(1, int(math.isqrt(n)) + 1) if n % d == 0)
    return pieces, padded * LANE, ny, n // ny


def nt_dot(a, b, precision=None):
    return lax.dot_general(
        a, b, (((1,), (1,)), ((), ())), preferred_element_type=F32, precision=precision
    )


def kernel(
    n,
    hidden_chunks,
    frozen_hbm,
    hidden_hbm,
    lengths_hbm,
    positives_hbm,
    down_hbm,
    up_hbm,
    gain_hbm,
    gdown_ref,
    gup_ref,
    loss_ref,
    frozen,
    hidden,
    down,
    lengths_ref,
    positives_ref,
    up_ref,
    gain_ref,
    state,
    own,
    land,
    both,
    sib,
    slots,
    res,
    load_sem,
    esend,
    erecv,
    fsend,
    frecv,
    ssend,
    srecv,
    rsend,
    rrecv,
    gsend,
    grecv,
):
    span, width = frozen.shape
    units = hidden.shape[1]
    rank = up_ref.shape[0]
    total = 2 * n
    rows = width // LANE
    pieces, cols, ny, nz = plan(n, width, units)
    pw = cols // pieces
    first_z = 1 if pieces > 1 else 0
    hu, hd = width // 2, units // 2
    dp = lax.axis_index("dp")
    mp = lax.axis_index("mp")
    other = 1 - mp
    me = dp * 2 + mp
    y = lax.rem(dp, ny)
    z = lax.div(dp, ny)

    cw = units // hidden_chunks
    loads = []
    for c in range(hidden_chunks):
        at = pl.ds(c * cw, cw)
        loads.append(
            (
                pltpu.make_async_copy(down_hbm.at[:, at], down.at[:, at], load_sem.at[1, c]),
                pltpu.make_async_copy(
                    hidden_hbm.at[0, :, at], hidden.at[:, at], load_sem.at[0, c]
                ),
            )
        )
    later = [
        pltpu.make_async_copy(src, dst, load_sem.at[2, i])
        for i, (src, dst) in enumerate(
            (
                (up_hbm, up_ref),
                (frozen_hbm.at[0], frozen),
                (gain_hbm, gain_ref),
                (lengths_hbm, lengths_ref),
                (positives_hbm, positives_ref),
            )
        )
    ]
    for pair in loads:
        for copy in pair:
            copy.start()
    for copy in later:
        copy.start()

    barrier = pltpu.get_barrier_semaphore()

    def greet(k, _):
        pl.semaphore_signal(
            barrier, inc=1, device_id={"dp": lax.rem(dp + k, n)}, device_id_type=MESH
        )
        return 0

    lax.fori_loop(1, n, greet, 0)
    pl.semaphore_signal(barrier, inc=1, device_id={"mp": other}, device_id_type=MESH)

    low = jnp.zeros((span, rank), F32)
    for c in range(hidden_chunks):
        for copy in loads[c]:
            copy.wait()
        at = pl.ds(c * cw, cw)
        low = low + nt_dot(hidden[:, at], down[:, at])
    low = low.astype(BF16)
    low_t = low.astype(F32).T.astype(BF16)
    for copy in later:
        copy.wait()

    tile = 512
    square = jnp.zeros((span, LANE), F32)
    for c in range(width // tile):
        at = pl.ds(c * tile, tile)
        s = frozen[:, at].astype(F32) + jnp.dot(
            low, up_ref[:, at], preferred_element_type=F32
        )
        state[:, at] = s
        for g in range(tile // LANE):
            part = s[:, g * LANE : (g + 1) * LANE]
            square = square + part * part
    inv = lax.rsqrt(jnp.sum(square, axis=1, keepdims=True) / width + EPS_NORM)
    length = lengths_ref[0]
    places = lax.broadcasted_iota(jnp.int32, (span, 1), 0)
    weight = jnp.where(places < length, 1.0, 0.0).astype(F32) / length.astype(F32)
    wi = weight * inv
    for r in range(rows):
        at = pl.ds(r * LANE, LANE)
        own[pl.ds(r, 1), :] = (
            jnp.sum(state[:, at] * wi, axis=0, keepdims=True) * gain_ref[:, at]
        )

    pl.semaphore_wait(barrier, n)

    def row(i):
        return pl.ds(pl.multiple_of(i * rows, rows), rows)

    def share(k):
        return pltpu.make_async_remote_copy(
            src_ref=own,
            dst_ref=land.at[row(me)],
            send_sem=esend.at[k],
            recv_sem=erecv.at[k],
            device_id={"dp": lax.rem(dp + k, n)},
            device_id_type=MESH,
        )

    def forward(k):
        peer = lax.rem(dp + n - k, n) * 2 + mp
        return pltpu.make_async_remote_copy(
            src_ref=land.at[row(peer)],
            dst_ref=land.at[row(peer)],
            send_sem=fsend.at[k],
            recv_sem=frecv.at[k],
            device_id={"mp": other},
            device_id_type=MESH,
        )

    def start_share(k, _):
        share(k).start()
        return 0

    lax.fori_loop(1, n, start_share, 0)
    land[row(me), :] = own[...]
    forward(0).start()

    def pass_on(k, _):
        share(k).wait_recv()
        forward(k).start()
        return 0

    lax.fori_loop(1, n, pass_on, 0)

    def arrive(k, _):
        forward(k).wait()
        return 0

    lax.fori_loop(0, n, arrive, 0)

    def sent(k, _):
        share(k).wait_send()
        return 0

    lax.fori_loop(1, n, sent, 0)

    ri = lax.broadcasted_iota(jnp.int32, (total, total), 0)
    ci = lax.broadcasted_iota(jnp.int32, (total, total), 1)
    eye = ri == ci
    if total <= 16:
        sums = [jnp.zeros((total, LANE), F32) for _ in range(total)]
        for r in range(rows):
            a = land[pl.ds(r, total, stride=rows), :]
            for j in range(total):
                sums[j] = sums[j] + a * a[j : j + 1, :]
        gram = jnp.zeros((total, total), F32)
        for j in range(total):
            gram = jnp.where(ci == j, jnp.sum(sums[j], axis=1, keepdims=True), gram)
    else:
        gram = jnp.zeros((total, total), F32)
        for r in range(rows):
            a = land[pl.ds(r, total, stride=rows), :]
            gram = gram + nt_dot(a, a, lax.Precision.HIGHEST)
    diag = jnp.where(eye, gram, 0.0)
    size_col = jnp.sqrt(jnp.sum(diag, axis=1, keepdims=True) + EPS_LEN)
    size_row = jnp.sqrt(jnp.sum(diag, axis=0, keepdims=True) + EPS_LEN)
    cosine = gram / size_col / size_row
    logits = cosine / TEMP
    masked = jnp.where(eye, -jnp.inf, logits)
    top = jnp.max(masked, axis=0, keepdims=True)
    lse = top + jnp.log(jnp.sum(jnp.exp(masked - top), axis=0, keepdims=True))
    target = ri == positives_ref[...]
    loss = lse - jnp.sum(jnp.where(target, logits, 0.0), axis=0, keepdims=True)
    loss_ref[0] = jnp.sum(loss) / total
    coef_t = jnp.where(eye, 0.0, jnp.exp(logits - lse)) - jnp.where(target, 1.0, 0.0)
    mine_row = jnp.sum(jnp.where(ri == me, coef_t, 0.0), axis=0, keepdims=True)
    picked = jnp.where(ci == me, coef_t, 0.0) + jnp.where(eye, mine_row, 0.0)
    m = jnp.sum(picked, axis=1, keepdims=True) / TEMP
    cos_me = jnp.sum(jnp.where(ci == me, cosine, 0.0), axis=1, keepdims=True)
    along = jnp.sum(m * cos_me, axis=0, keepdims=True)
    is_me = ri[:, 0:1] == me
    size_me = jnp.sum(jnp.where(is_me, size_col, 0.0), axis=0, keepdims=True)
    q = (m - jnp.where(is_me, along, 0.0)) / size_col / size_me

    scaled = []
    inner = jnp.zeros((span, LANE), F32)
    for r in range(rows):
        at = pl.ds(r * LANE, LANE)
        a = land[pl.ds(r, total, stride=rows), :]
        sc = jnp.sum(a * q, axis=0, keepdims=True) * gain_ref[:, at]
        scaled.append(sc)
        inner = inner + state[:, at] * sc
    inner = jnp.sum(inner, axis=1, keepdims=True) * weight / width
    back = inv * inv * inv * inner
    dlow = jnp.zeros((span, rank), F32)
    per = tile // LANE
    for c in range(width // tile):
        at = pl.ds(c * tile, tile)
        sc = jnp.concatenate(scaled[c * per : (c + 1) * per], axis=1)
        ds = (wi * sc - state[:, at] * back).astype(BF16)
        dlow = dlow + nt_dot(ds, up_ref[:, at])
        half, col = divmod(c * tile, hu)
        both[half, :, pl.ds(col, tile)] = jnp.dot(low_t, ds, preferred_element_type=F32)
    dlow_t = dlow.astype(BF16).astype(F32).T.astype(BF16)

    def compute_piece(p, half):
        lo, hi = max(p * pw, hu), min((p + 1) * pw, hu + hd)
        while lo < hi:
            w = min(1024, hi - lo)
            at = pl.ds(pl.multiple_of(half * hd + (lo - hu), LANE), w)
            both[half, :, pl.ds(lo, w)] = jnp.dot(
                dlow_t, hidden[:, at], preferred_element_type=F32
            )
            lo += w
        lo = max(p * pw, hu + hd)
        if lo < (p + 1) * pw:
            both[half, :, pl.ds(lo, (p + 1) * pw - lo)] = jnp.zeros(
                (rank, (p + 1) * pw - lo), F32
            )

    waits = []

    def start(copy):
        copy.start()
        waits.append(copy)

    def to_sibling(p):
        at = pl.ds(p * pw, pw)
        return pltpu.make_async_remote_copy(
            src_ref=both.at[other, :, at],
            dst_ref=sib.at[:, at],
            send_sem=ssend.at[p],
            recv_sem=srecv.at[p],
            device_id={"mp": other},
            device_id_type=MESH,
        )

    along_y = (ny, y, lambda to: z * ny + to)
    along_z = (nz, z, lambda to: to * ny + y)

    def axes(p):
        return (along_z, along_y) if p < first_z else (along_y, along_z)

    def span_of(p, level):
        base, size = p * pw, pw
        for places, place, _ in axes(p)[:level]:
            size = size // places
            base = base + place * size
        return base, size

    def chunk(base, size, index):
        return pl.ds(pl.multiple_of(base + index * size, LANE), size)

    def scatter(p, level, k):
        places, place, device = axes(p)[level]
        base, size = span_of(p, level)
        to = lax.rem(place + k, places)
        size = size // places
        return pltpu.make_async_remote_copy(
            src_ref=both.at[mp, :, chunk(base, size, to)],
            dst_ref=slots.at[p, level, k - 1, :, pl.ds(0, size)],
            send_sem=rsend.at[p, level, k - 1],
            recv_sem=rrecv.at[p, level, k - 1],
            device_id={"dp": device(to)},
            device_id_type=MESH,
        )

    def gather(p, level, k):
        places, place, device = axes(p)[level]
        base, size = span_of(p, level)
        to = lax.rem(place + k, places)
        size = size // places
        at = chunk(base, size, place)
        return pltpu.make_async_remote_copy(
            src_ref=res.at[:, at],
            dst_ref=res.at[:, at],
            send_sem=gsend.at[p, level, k - 1],
            recv_sem=grecv.at[p, level, k - 1],
            device_id={"dp": device(to)},
            device_id_type=MESH,
        )

    def others(p, level):
        return range(1, axes(p)[level][0])

    def reduce(p, level):
        base, size = span_of(p, level + 1)
        at = chunk(base, size, 0)
        acc = both[mp, :, at]
        for k in others(p, level):
            scatter(p, level, k).wait_recv()
            acc = acc + slots[p, level, k - 1, :, pl.ds(0, size)]
        return at, acc

    for p in range(pieces):
        compute_piece(p, other)
        start(to_sibling(p))
    for p in range(pieces):
        compute_piece(p, mp)
        to_sibling(p).wait_recv()
        at = pl.ds(p * pw, pw)
        both[mp, :, at] = both[mp, :, at] + sib[:, at]
        for k in others(p, 0):
            start(scatter(p, 0, k))
    order = list(range(first_z, pieces)) + list(range(first_z))
    for p in order:
        at, acc = reduce(p, 0)
        both[mp, :, at] = acc
        for k in others(p, 1):
            start(scatter(p, 1, k))
    for p in order[::-1]:
        at, acc = reduce(p, 1)
        res[:, at] = acc
        for k in others(p, 1):
            start(gather(p, 1, k))
    for p in order[::-1]:
        for k in others(p, 1):
            gather(p, 1, k).wait_recv()
        for k in others(p, 0):
            start(gather(p, 0, k))
    for p in range(pieces):
        for k in others(p, 0):
            gather(p, 0, k).wait_recv()
        lo, hi = p * pw, min((p + 1) * pw, hu)
        if lo < hi:
            gup_ref[:, pl.ds(lo, hi - lo)] = res[:, pl.ds(lo, hi - lo)]
        lo, hi = max(p * pw, hu), min((p + 1) * pw, hu + hd)
        if lo < hi:
            gdown_ref[:, pl.ds(lo - hu, hi - lo)] = res[:, pl.ds(lo, hi - lo)]
    for copy in waits:
        copy.wait_send()


def body(
    frozen_state,
    gated_hidden,
    lengths,
    positives,
    adapter_down_factor,
    adapter_up_factor,
    final_norm_weight,
    *,
    n,
):
    _, span, width = frozen_state.shape
    units = gated_hidden.shape[2]
    rank = adapter_down_factor.shape[0]
    total = positives.shape[0]
    pieces, cols, ny, nz = plan(n, width, units)
    least, most = max(min(ny, nz), 1), max(ny, nz, 2)
    chunks = 7
    dma = pltpu.SemaphoreType.DMA
    vmem = pl.BlockSpec(memory_space=pltpu.VMEM)
    smem = pl.BlockSpec(memory_space=pltpu.SMEM)
    hbm = pl.BlockSpec(memory_space=pl.ANY)
    grad_down, grad_up, mean_loss = pl.pallas_call(
        functools.partial(kernel, n, chunks),
        out_shape=(
            jax.ShapeDtypeStruct((rank, units // 2), F32),
            jax.ShapeDtypeStruct((rank, width // 2), F32),
            jax.ShapeDtypeStruct((1,), F32),
        ),
        in_specs=[hbm] * 7,
        out_specs=(vmem, vmem, smem),
        scratch_shapes=[
            pltpu.VMEM((span, width), BF16),
            pltpu.VMEM((span, units), BF16),
            pltpu.VMEM((rank, units), BF16),
            pltpu.SMEM((1,), jnp.int32),
            pltpu.VMEM((1, total), jnp.int32),
            pltpu.VMEM((rank, width), BF16),
            pltpu.VMEM((1, width), F32),
            pltpu.VMEM((span, width), F32),
            pltpu.VMEM((width // LANE, LANE), F32),
            pltpu.VMEM((total * (width // LANE), LANE), F32),
            pltpu.VMEM((2, rank, cols), F32),
            pltpu.VMEM((rank, cols), F32),
            pltpu.VMEM((pieces, 2, most - 1, rank, cols // pieces // least), F32),
            pltpu.VMEM((rank, cols), F32),
            dma((3, max(chunks, 5))),
            dma((n,)),
            dma((n,)),
            dma((n,)),
            dma((n,)),
            dma((pieces,)),
            dma((pieces,)),
            dma((pieces, 2, most - 1)),
            dma((pieces, 2, most - 1)),
            dma((pieces, 2, most - 1)),
            dma((pieces, 2, most - 1)),
        ],
        compiler_params=pltpu.CompilerParams(
            collective_id=0, has_side_effects=True, vmem_limit_bytes=60 * 2**20
        ),
    )(
        frozen_state,
        gated_hidden,
        lengths,
        positives.reshape(1, total),
        adapter_down_factor,
        adapter_up_factor,
        final_norm_weight.reshape(1, width),
    )
    return grad_down, grad_up, mean_loss


def solution(mesh):
    in_specs = (
        P(("groups", "dp", "mp"), None, None),
        P(("groups", "dp", "mp"), None, None),
        P(("groups", "dp", "mp")),
        P("groups"),
        P(),
        P(),
        P(),
    )
    out_specs = (P("groups", "mp"), P("groups", "mp"), P("groups"))
    return jax.shard_map(
        functools.partial(body, n=mesh.shape["dp"]),
        mesh=mesh,
        in_specs=in_specs,
        out_specs=out_specs,
        check_vma=False,
    )
```

```python
import functools
import math

import jax
import jax.numpy as jnp
from jax import lax
from jax.experimental import pallas as pl
from jax.experimental.pallas import tpu as pltpu
from jax.sharding import PartitionSpec as P

EPS_NORM = 1e-05
EPS_LEN = 1e-06
TEMP = 0.05
LANE = 128
MESH = pl.DeviceIdType.MESH
F32 = jnp.float32
BF16 = jnp.bfloat16


def plan(n, width, hidden):
    per = -(-(width + hidden) // 2 // LANE // n)
    if per >= 9:
        first, second = 3 * per // 9, 3 * per // 9
        parts = (first, second, per - first - second)
    else:
        parts = (per,)
    ny = max(d for d in range(1, int(math.isqrt(n)) + 1) if n % d == 0)
    return tuple(w * n * LANE for w in parts), ny, n // ny


STEPS = {
    1: (("sib", 0), ("s0", 0), ("r0", 0), ("r1", 0), ("g1", 0), ("out", 0)),
    3: (
        ("sib", 0), ("s0", 0), ("sib", 1), ("s0", 1), ("sib", 2), ("s0", 2),
        ("r0", 1), ("r0", 0), ("r0", 2),
        ("r1", 0), ("r1", 1), ("r1", 2),
        ("g1", 1), ("g1", 0), ("g1", 2),
        ("out", 1), ("out", 0), ("out", 2),
    ),
}


def nt_dot(a, b, precision=None):
    return lax.dot_general(
        a, b, (((1,), (1,)), ((), ())), preferred_element_type=F32, precision=precision
    )


def kernel(
    n,
    hidden_chunks,
    frozen_hbm,
    hidden_hbm,
    lengths_hbm,
    positives_hbm,
    down_hbm,
    up_hbm,
    gain_hbm,
    gdown_hbm,
    gup_hbm,
    loss_ref,
    frozen,
    hidden,
    down,
    lengths_ref,
    positives_ref,
    up_ref,
    gain_ref,
    state,
    own,
    land,
    both,
    sib,
    slots,
    res,
    load_sem,
    esend,
    erecv,
    fsend,
    frecv,
    ssend,
    srecv,
    rsend,
    rrecv,
    gsend,
    grecv,
    osem,
):
    span, width = frozen.shape
    units = hidden.shape[1]
    rank = up_ref.shape[0]
    total = 2 * n
    rows = width // LANE
    widths, ny, nz = plan(n, width, units)
    pieces = len(widths)
    bases = [sum(widths[:p]) for p in range(pieces)]
    first_z = 1 if pieces > 1 else 0
    hu, hd = width // 2, units // 2
    dp = lax.axis_index("dp")
    mp = lax.axis_index("mp")
    other = 1 - mp
    me = dp * 2 + mp
    y = lax.rem(dp, ny)
    z = lax.div(dp, ny)

    cw = units // hidden_chunks
    loads = []
    for c in range(hidden_chunks):
        at = pl.ds(c * cw, cw)
        loads.append(
            (
                pltpu.make_async_copy(down_hbm.at[:, at], down.at[:, at], load_sem.at[1, c]),
                pltpu.make_async_copy(
                    hidden_hbm.at[0, :, at], hidden.at[:, at], load_sem.at[0, c]
                ),
            )
        )
    later = [
        pltpu.make_async_copy(src, dst, load_sem.at[2, i])
        for i, (src, dst) in enumerate(
            (
                (up_hbm, up_ref),
                (frozen_hbm.at[0], frozen),
                (gain_hbm, gain_ref),
                (lengths_hbm, lengths_ref),
                (positives_hbm, positives_ref),
            )
        )
    ]
    for pair in loads:
        for copy in pair:
            copy.start()
    for copy in later:
        copy.start()

    barrier = pltpu.get_barrier_semaphore()

    def greet(k, _):
        pl.semaphore_signal(
            barrier, inc=1, device_id={"dp": lax.rem(dp + k, n)}, device_id_type=MESH
        )
        return 0

    lax.fori_loop(1, n, greet, 0)
    pl.semaphore_signal(barrier, inc=1, device_id={"mp": other}, device_id_type=MESH)

    low = jnp.zeros((span, rank), F32)
    for c in range(hidden_chunks):
        for copy in loads[c]:
            copy.wait()
        at = pl.ds(c * cw, cw)
        low = low + nt_dot(hidden[:, at], down[:, at])
    low = low.astype(BF16)
    low_t = low.astype(F32).T.astype(BF16)
    for copy in later:
        copy.wait()

    tile = 512
    square = jnp.zeros((span, LANE), F32)
    for c in range(width // tile):
        at = pl.ds(c * tile, tile)
        s = frozen[:, at].astype(F32) + jnp.dot(
            low, up_ref[:, at], preferred_element_type=F32
        )
        state[:, at] = s
        for g in range(tile // LANE):
            part = s[:, g * LANE : (g + 1) * LANE]
            square = square + part * part
    inv = lax.rsqrt(jnp.sum(square, axis=1, keepdims=True) / width + EPS_NORM)
    length = lengths_ref[0]
    places = lax.broadcasted_iota(jnp.int32, (span, 1), 0)
    weight = jnp.where(places < length, 1.0, 0.0).astype(F32) / length.astype(F32)
    wi = weight * inv
    for r in range(rows):
        at = pl.ds(r * LANE, LANE)
        own[pl.ds(r, 1), :] = (
            jnp.sum(state[:, at] * wi, axis=0, keepdims=True) * gain_ref[:, at]
        )

    pl.semaphore_wait(barrier, n)

    def row(i):
        return pl.ds(pl.multiple_of(i * rows, rows), rows)

    def share(k):
        return pltpu.make_async_remote_copy(
            src_ref=own,
            dst_ref=land.at[row(me)],
            send_sem=esend.at[k],
            recv_sem=erecv.at[k],
            device_id={"dp": lax.rem(dp + k, n)},
            device_id_type=MESH,
        )

    def forward(k):
        peer = lax.rem(dp + n - k, n) * 2 + mp
        return pltpu.make_async_remote_copy(
            src_ref=land.at[row(peer)],
            dst_ref=land.at[row(peer)],
            send_sem=fsend.at[k],
            recv_sem=frecv.at[k],
            device_id={"mp": other},
            device_id_type=MESH,
        )

    def start_share(k, _):
        share(k).start()
        return 0

    lax.fori_loop(1, n, start_share, 0)
    land[row(me), :] = own[...]
    forward(0).start()

    def pass_on(k, _):
        share(k).wait_recv()
        forward(k).start()
        return 0

    lax.fori_loop(1, n, pass_on, 0)

    def arrive(k, _):
        forward(k).wait()
        return 0

    lax.fori_loop(0, n, arrive, 0)

    def sent(k, _):
        share(k).wait_send()
        return 0

    lax.fori_loop(1, n, sent, 0)

    ri = lax.broadcasted_iota(jnp.int32, (total, total), 0)
    ci = lax.broadcasted_iota(jnp.int32, (total, total), 1)
    eye = ri == ci
    if total <= 16:
        sums = [jnp.zeros((total, LANE), F32) for _ in range(total)]
        for r in range(rows):
            a = land[pl.ds(r, total, stride=rows), :]
            for j in range(total):
                sums[j] = sums[j] + a * a[j : j + 1, :]
        gram = jnp.zeros((total, total), F32)
        for j in range(total):
            gram = jnp.where(ci == j, jnp.sum(sums[j], axis=1, keepdims=True), gram)
    else:
        gram = jnp.zeros((total, total), F32)
        for r in range(rows):
            a = land[pl.ds(r, total, stride=rows), :]
            gram = gram + nt_dot(a, a, lax.Precision.HIGHEST)
    diag = jnp.where(eye, gram, 0.0)
    size_col = jnp.sqrt(jnp.sum(diag, axis=1, keepdims=True) + EPS_LEN)
    size_row = jnp.sqrt(jnp.sum(diag, axis=0, keepdims=True) + EPS_LEN)
    cosine = gram / size_col / size_row
    logits = cosine / TEMP
    masked = jnp.where(eye, -jnp.inf, logits)
    top = jnp.max(masked, axis=0, keepdims=True)
    lse = top + jnp.log(jnp.sum(jnp.exp(masked - top), axis=0, keepdims=True))
    target = ri == positives_ref[...]
    loss = lse - jnp.sum(jnp.where(target, logits, 0.0), axis=0, keepdims=True)
    loss_ref[0] = jnp.sum(loss) / total
    coef_t = jnp.where(eye, 0.0, jnp.exp(logits - lse)) - jnp.where(target, 1.0, 0.0)
    mine_row = jnp.sum(jnp.where(ri == me, coef_t, 0.0), axis=0, keepdims=True)
    picked = jnp.where(ci == me, coef_t, 0.0) + jnp.where(eye, mine_row, 0.0)
    m = jnp.sum(picked, axis=1, keepdims=True) / TEMP
    cos_me = jnp.sum(jnp.where(ci == me, cosine, 0.0), axis=1, keepdims=True)
    along = jnp.sum(m * cos_me, axis=0, keepdims=True)
    is_me = ri[:, 0:1] == me
    size_me = jnp.sum(jnp.where(is_me, size_col, 0.0), axis=0, keepdims=True)
    q = (m - jnp.where(is_me, along, 0.0)) / size_col / size_me

    scaled = []
    inner = jnp.zeros((span, LANE), F32)
    for r in range(rows):
        at = pl.ds(r * LANE, LANE)
        a = land[pl.ds(r, total, stride=rows), :]
        sc = jnp.sum(a * q, axis=0, keepdims=True) * gain_ref[:, at]
        scaled.append(sc)
        inner = inner + state[:, at] * sc
    inner = jnp.sum(inner, axis=1, keepdims=True) * weight / width
    back = inv * inv * inv * inner
    dlow = jnp.zeros((span, rank), F32)
    per = tile // LANE
    for c in range(width // tile):
        at = pl.ds(c * tile, tile)
        sc = jnp.concatenate(scaled[c * per : (c + 1) * per], axis=1)
        ds = (wi * sc - state[:, at] * back).astype(BF16)
        dlow = dlow + nt_dot(ds, up_ref[:, at])
        half, col = divmod(c * tile, hu)
        both[half, :, pl.ds(col, tile)] = jnp.dot(low_t, ds, preferred_element_type=F32)
    dlow_t = dlow.astype(BF16).astype(F32).T.astype(BF16)

    def compute_piece(p, half):
        end = bases[p] + widths[p]
        lo, hi = max(bases[p], hu), min(end, hu + hd)
        while lo < hi:
            w = min(1024, hi - lo)
            at = pl.ds(pl.multiple_of(half * hd + (lo - hu), LANE), w)
            both[half, :, pl.ds(lo, w)] = jnp.dot(
                dlow_t, hidden[:, at], preferred_element_type=F32
            )
            lo += w
        lo = max(bases[p], hu + hd)
        if lo < end:
            both[half, :, pl.ds(lo, end - lo)] = jnp.zeros((rank, end - lo), F32)

    waits = []

    def start(copy):
        copy.start()
        waits.append(copy)

    def to_sibling(p):
        at = pl.ds(bases[p], widths[p])
        return pltpu.make_async_remote_copy(
            src_ref=both.at[other, :, at],
            dst_ref=sib.at[:, at],
            send_sem=ssend.at[p],
            recv_sem=srecv.at[p],
            device_id={"mp": other},
            device_id_type=MESH,
        )

    along_y = (ny, y, lambda to: z * ny + to)
    along_z = (nz, z, lambda to: to * ny + y)

    def axes(p):
        return (along_z, along_y) if p < first_z else (along_y, along_z)

    def span_of(p, level):
        base, size = bases[p], widths[p]
        for places, place, _ in axes(p)[:level]:
            size = size // places
            base = base + place * size
        return base, size

    def chunk(base, size, index):
        return pl.ds(pl.multiple_of(base + index * size, LANE), size)

    def scatter(p, level, k):
        places, place, device = axes(p)[level]
        base, size = span_of(p, level)
        to = lax.rem(place + k, places)
        size = size // places
        return pltpu.make_async_remote_copy(
            src_ref=both.at[mp, :, chunk(base, size, to)],
            dst_ref=slots.at[p, level, k - 1, :, pl.ds(0, size)],
            send_sem=rsend.at[p, level, k - 1],
            recv_sem=rrecv.at[p, level, k - 1],
            device_id={"dp": device(to)},
            device_id_type=MESH,
        )

    def gather(p, level, k):
        places, place, device = axes(p)[level]
        base, size = span_of(p, level)
        to = lax.rem(place + k, places)
        size = size // places
        at = chunk(base, size, place)
        return pltpu.make_async_remote_copy(
            src_ref=res.at[:, at],
            dst_ref=res.at[:, at],
            send_sem=gsend.at[p, level, k - 1],
            recv_sem=grecv.at[p, level, k - 1],
            device_id={"dp": device(to)},
            device_id_type=MESH,
        )

    def others(p, level):
        return range(1, axes(p)[level][0])

    def reduce(p, level):
        base, size = span_of(p, level + 1)
        at = chunk(base, size, 0)
        acc = both[mp, :, at]
        for k in others(p, level):
            scatter(p, level, k).wait_recv()
            acc = acc + slots[p, level, k - 1, :, pl.ds(0, size)]
        return at, acc

    out_copies = []

    def write_out(p):
        end = bases[p] + widths[p]
        for c, (ref, first, last) in enumerate(
            ((gup_hbm, 0, hu), (gdown_hbm, hu, hu + hd))
        ):
            lo, hi = max(bases[p], first), min(end, last)
            if lo < hi:
                copy = pltpu.make_async_copy(
                    res.at[:, pl.ds(lo, hi - lo)],
                    ref.at[:, pl.ds(lo - first, hi - lo)],
                    osem.at[p, c],
                )
                copy.start()
                out_copies.append(copy)

    for p in range(pieces):
        compute_piece(p, other)
        start(to_sibling(p))
    for step, p in STEPS[pieces]:
        if step == "sib":
            compute_piece(p, mp)
            to_sibling(p).wait_recv()
            at = pl.ds(bases[p], widths[p])
            both[mp, :, at] = both[mp, :, at] + sib[:, at]
        elif step == "s0":
            for k in others(p, 0):
                start(scatter(p, 0, k))
        elif step == "r0":
            at, acc = reduce(p, 0)
            both[mp, :, at] = acc
            for k in others(p, 1):
                start(scatter(p, 1, k))
        elif step == "r1":
            at, acc = reduce(p, 1)
            res[:, at] = acc
            for k in others(p, 1):
                start(gather(p, 1, k))
        elif step == "g1":
            for k in others(p, 1):
                gather(p, 1, k).wait_recv()
            for k in others(p, 0):
                start(gather(p, 0, k))
        else:
            for k in others(p, 0):
                gather(p, 0, k).wait_recv()
            write_out(p)
    for copy in waits:
        copy.wait_send()
    for copy in out_copies:
        copy.wait()


def body(
    frozen_state,
    gated_hidden,
    lengths,
    positives,
    adapter_down_factor,
    adapter_up_factor,
    final_norm_weight,
    *,
    n,
):
    _, span, width = frozen_state.shape
    units = gated_hidden.shape[2]
    rank = adapter_down_factor.shape[0]
    total = positives.shape[0]
    widths, ny, nz = plan(n, width, units)
    pieces, cols = len(widths), sum(widths)
    least, most = max(min(ny, nz), 1), max(ny, nz, 2)
    chunks = 7
    dma = pltpu.SemaphoreType.DMA
    smem = pl.BlockSpec(memory_space=pltpu.SMEM)
    hbm = pl.BlockSpec(memory_space=pl.ANY)
    grad_down, grad_up, mean_loss = pl.pallas_call(
        functools.partial(kernel, n, chunks),
        out_shape=(
            jax.ShapeDtypeStruct((rank, units // 2), F32),
            jax.ShapeDtypeStruct((rank, width // 2), F32),
            jax.ShapeDtypeStruct((1,), F32),
        ),
        in_specs=[hbm] * 7,
        out_specs=(hbm, hbm, smem),
        scratch_shapes=[
            pltpu.VMEM((span, width), BF16),
            pltpu.VMEM((span, units), BF16),
            pltpu.VMEM((rank, units), BF16),
            pltpu.SMEM((1,), jnp.int32),
            pltpu.VMEM((1, total), jnp.int32),
            pltpu.VMEM((rank, width), BF16),
            pltpu.VMEM((1, width), F32),
            pltpu.VMEM((span, width), F32),
            pltpu.VMEM((width // LANE, LANE), F32),
            pltpu.VMEM((total * (width // LANE), LANE), F32),
            pltpu.VMEM((2, rank, cols), F32),
            pltpu.VMEM((rank, cols), F32),
            pltpu.VMEM((pieces, 2, most - 1, rank, max(widths) // least), F32),
            pltpu.VMEM((rank, cols), F32),
            dma((3, max(chunks, 5))),
            dma((n,)),
            dma((n,)),
            dma((n,)),
            dma((n,)),
            dma((pieces,)),
            dma((pieces,)),
            dma((pieces, 2, most - 1)),
            dma((pieces, 2, most - 1)),
            dma((pieces, 2, most - 1)),
            dma((pieces, 2, most - 1)),
            dma((pieces, 2)),
        ],
        compiler_params=pltpu.CompilerParams(
            collective_id=0, has_side_effects=True, vmem_limit_bytes=60 * 2**20
        ),
    )(
        frozen_state,
        gated_hidden,
        lengths,
        positives.reshape(1, total),
        adapter_down_factor,
        adapter_up_factor,
        final_norm_weight.reshape(1, width),
    )
    return grad_down, grad_up, mean_loss


def solution(mesh):
    in_specs = (
        P(("groups", "dp", "mp"), None, None),
        P(("groups", "dp", "mp"), None, None),
        P(("groups", "dp", "mp")),
        P("groups"),
        P(),
        P(),
        P(),
    )
    out_specs = (P("groups", "mp"), P("groups", "mp"), P("groups"))
    return jax.shard_map(
        functools.partial(body, n=mesh.shape["dp"]),
        mesh=mesh,
        in_specs=in_specs,
        out_specs=out_specs,
        check_vma=False,
    )
```
